32 devices in a mesh: row: 8 (over z, core), col: 4 (over y, x).
Axes of the slice: x: 2, y: 2, z: 4, core: 2. Of those that a mesh axis runs over, the one named last changes fastest.
Arguments:
- trailing: float32 [4096, 4096], P('row', 'col'), may hold values from -6 to 6
- panel: float32 [4096, 512], P(('row', 'col')), may hold values from -0.25 to 0.25
- inv_factor: float32 [512, 512], P(None, 'col'), as said below
- later_series: float32 [4096, 1024], P('row', 'col'), may hold values from -6 to 6
- fold_series: float32 [512, 1024], P('row', 'col'), may hold values from -6 to 6
- fold_len: int32 [1024], P('col'), may hold values from 1 to 8, as said below
Outputs:
- new_trailing: float32 [4096, 4096], P('row', 'col')
- new_series: float32 [4096, 1024], P('row', 'col')
The draws below stay inside these ranges and needn't reach their ends.
Inputs may be any that keep to these rules, and one draw needn't show every extreme that they name: inv_factor is lower triangular with a diagonal between 1 and 2. `fold_len`: some series reach all 8 blocks and some only one.
All inputs are finite; a program needn't handle non-finite values.
Results may differ from the reference program's by a relative error of at most 0.0003.
Values sent between devices are 32-bit elements; how exact they have to be, the bound alone decides.
A program may use at most 64 MiB of HBM per device.

```python
import math
import jax
import jax.numpy as jnp
from jax import lax

PANEL = 512
SERIES = 1024
ORDER = 4096
BLOCKS = 8


def draw_inv_factor(key, part):
    inner = jax.random.fold_in(key, 7)
    first, second = jax.random.split(inner)
    diag_part = jax.random.uniform(first, (PANEL,), jnp.float32, 1.0, 2.0)
    spread = 0.6 / math.sqrt(PANEL)
    lower = jnp.tril(jax.random.normal(second, (PANEL, PANEL), jnp.float32) * spread, -1)
    return lower + jnp.diag(diag_part)


def draw_fold_len(key, part):
    inner = jax.random.fold_in(key, 11)
    values = jax.random.randint(inner, (SERIES,), 1, BLOCKS + 1, dtype=jnp.int32)
    return values.at[0].set(BLOCKS).at[1].set(1)


def block_levels(stream_key, shape, pieces, low, top_value):
    factor_of = 1.0
    for position, shards_of in pieces:
        draws = jax.random.uniform(jax.random.fold_in(jax.random.fold_in(stream_key, 6), position), (shards_of,), jnp.float32, low / len(pieces), top_value / len(pieces))
        factor_of = factor_of * jnp.repeat(jnp.exp(draws), shape[position] // shards_of).reshape((-1,) + (1,) * (len(shape) - 1 - position))
    return factor_of


def noise(rng, shape, width, most, cuts=(), kind=jnp.bfloat16):
    values = width * jax.random.normal(rng, shape, jnp.float32)
    if cuts:
        values = values * block_levels(rng, shape, cuts, -0.22, 0.18)
    return jnp.clip(values, -most, most).astype(kind)


def setup_inputs(seed: int = 0) -> dict:
    keys = jax.random.split(jax.random.key(seed), 7)
    return {
        "trailing": noise(keys[0], (ORDER, ORDER), 1.0, 6.0, ((0, 8), (1, 4)), jnp.float32),
        "panel": noise(keys[1], (ORDER, PANEL), PANEL ** -0.5, 0.25, ((0, 32),), jnp.float32),
        "inv_factor": draw_inv_factor(jax.random.fold_in(keys[6], 71), 0),
        "later_series": noise(keys[3], (ORDER, SERIES), 1.0, 6.0, ((0, 8), (1, 4)), jnp.float32),
        "fold_series": noise(keys[4], (PANEL, SERIES), 1.0, 6.0, ((0, 8), (1, 4)), jnp.float32),
        "fold_len": draw_fold_len(jax.random.fold_in(keys[6], 71), 0),
    }


def reference(trailing, panel, inv_factor, later_series, fold_series, fold_len):
    highest = lax.Precision.HIGHEST
    solved = jnp.dot(panel, inv_factor.T, precision=highest, preferred_element_type=jnp.float32)
    order = trailing.shape[0]
    blocks = order // PANEL
    column_tile = jnp.arange(order, dtype=jnp.int32) // PANEL

    def one_block(item):
        rows, solved_rows, index = item
        update = jnp.dot(solved_rows, solved.T, precision=highest, preferred_element_type=jnp.float32)
        return jnp.where(column_tile[None, :] <= index, rows - update, rows)

    new_trailing = lax.map(one_block, (trailing.reshape(blocks, PANEL, order), solved.reshape(blocks, PANEL, PANEL), jnp.arange(blocks, dtype=jnp.int32))).reshape(order, order)
    innovations = jnp.dot(inv_factor, fold_series, precision=highest, preferred_element_type=jnp.float32)
    correction = jnp.dot(solved, innovations, precision=highest, preferred_element_type=jnp.float32)
    row_tile = jnp.arange(order, dtype=jnp.int32) // PANEL
    active = row_tile[:, None] < fold_len[None, :]
    new_series = jnp.where(active, later_series - correction, later_series)
    return new_trailing, new_series
```

```python
import functools

import jax
import jax.numpy as jnp
from jax import lax
from jax.experimental import pallas as pl
from jax.experimental.pallas import tpu as pltpu
from jax.sharding import PartitionSpec as P

MESH = pl.DeviceIdType.MESH
F32 = jnp.float32
BF16 = jnp.bfloat16
NT = (((1,), (1,)), ((), ()))
NN = (((1,), (0,)), ((), ()))


def split(x):
    high = x.astype(BF16)
    return high, (x - high.astype(F32)).astype(BF16)


def dot3(a, b, dims):
    dot = functools.partial(lax.dot_general, dimension_numbers=dims, preferred_element_type=F32)
    return dot(a[0], b[0]) + (dot(a[0], b[1]) + dot(a[1], b[0]))


def kernel(
    planes, groups, chunks,
    panel_ref, inv_ref, fold_ref,
    update_ref, corr_ref,
    tiles, inv_t, fold, q_hi, q_lo, g_hi, g_lo,
    rb_send, rb_recv, up_send, up_recv, sib_send, sib_recv,
    fold_send, fold_recv, fsib_send, fsib_recv,
    inv_send, inv_recv, isib_send, isib_recv,
):
    row = lax.axis_index("row")
    c = lax.axis_index("col")
    z = row // 2
    k = row % 2
    piece = panel_ref.shape[0]
    step = piece // chunks
    width = panel_ref.shape[1]
    fold_rows = fold_ref.shape[0]
    inv_cols = inv_ref.shape[1]
    half = inv_cols // 2
    sibling = (2 * z + (1 - k), c)

    barrier = pltpu.get_barrier_semaphore()
    pl.semaphore_signal(barrier, inc=1, device_id=sibling, device_id_type=MESH)
    for o in range(1, planes):
        pl.semaphore_signal(
            barrier, inc=1, device_id=(2 * ((z + o) % planes) + k, c), device_id_type=MESH
        )
    for o in range(1, groups):
        pl.semaphore_signal(
            barrier, inc=1, device_id=(row, (c + o) % groups), device_id_type=MESH
        )

    def slot_of(col):
        return jnp.where(col == z, k, 2)

    slot = slot_of(c)

    def rows_of(j, h):
        return pl.ds(pl.multiple_of(j * piece + h * step, step), step)

    def rb_copy(o, h):
        target = (c + o) % groups
        return pltpu.make_async_remote_copy(
            src_ref=tiles.at[slot, rows_of(c, h)],
            dst_ref=tiles.at[slot_of(target), rows_of(c, h)],
            send_sem=rb_send.at[o, h],
            recv_sem=rb_recv.at[c, h],
            device_id=(row, target),
            device_id_type=MESH,
        )

    def rb_arrival(j, h):
        return pltpu.make_async_remote_copy(
            src_ref=tiles.at[slot, rows_of(j, h)],
            dst_ref=tiles.at[slot, rows_of(j, h)],
            send_sem=rb_send.at[0, h],
            recv_sem=rb_recv.at[j, h],
            device_id=sibling,
            device_id_type=MESH,
        )

    def up_copy(j, h):
        return pltpu.make_async_remote_copy(
            src_ref=tiles.at[k, rows_of(j, h)],
            dst_ref=tiles.at[k, rows_of(j, h)],
            send_sem=up_send.at[j, h],
            recv_sem=up_recv.at[j, h],
            device_id=(jnp.minimum(row + 2, 2 * planes - 2 + k), c),
            device_id_type=MESH,
        )

    def sib_copy(tile, j, h):
        return pltpu.make_async_remote_copy(
            src_ref=tiles.at[tile, rows_of(j, h)],
            dst_ref=tiles.at[tile, rows_of(j, h)],
            send_sem=sib_send.at[j, h],
            recv_sem=sib_recv.at[j, h],
            device_id=sibling,
            device_id_type=MESH,
        )

    def fold_at(plane, core):
        return fold.at[pl.ds(pl.multiple_of((2 * plane + core) * fold_rows, fold_rows), fold_rows)]

    def fold_copy(o):
        target = (z + o) % planes
        return pltpu.make_async_remote_copy(
            src_ref=fold_at(z, k),
            dst_ref=fold_at(z, k),
            send_sem=fold_send.at[o],
            recv_sem=fold_recv.at[planes - o],
            device_id=(2 * target + k, c),
            device_id_type=MESH,
        )

    def fold_arrival(o):
        ref = fold_at((z + o) % planes, k)
        return pltpu.make_async_remote_copy(
            src_ref=ref, dst_ref=ref, send_sem=fold_send.at[0], recv_sem=fold_recv.at[o],
            device_id=sibling, device_id_type=MESH,
        )

    def fsib_copy(o, core):
        ref = fold_at((z + o) % planes, core)
        return pltpu.make_async_remote_copy(
            src_ref=ref, dst_ref=ref, send_sem=fsib_send.at[o], recv_sem=fsib_recv.at[o],
            device_id=sibling, device_id_type=MESH,
        )

    def inv_at(col, core):
        return inv_t.at[pl.ds(pl.multiple_of(col * inv_cols + core * half, half), half)]

    def inv_copy(o):
        return pltpu.make_async_remote_copy(
            src_ref=inv_at(c, k),
            dst_ref=inv_at(c, k),
            send_sem=inv_send.at[o],
            recv_sem=inv_recv.at[groups - o],
            device_id=(row, (c + o) % groups),
            device_id_type=MESH,
        )

    def inv_arrival(o):
        ref = inv_at((c + o) % groups, k)
        return pltpu.make_async_remote_copy(
            src_ref=ref, dst_ref=ref, send_sem=inv_send.at[0], recv_sem=inv_recv.at[o],
            device_id=sibling, device_id_type=MESH,
        )

    def isib_copy(o, core):
        ref = inv_at((c + o) % groups, core)
        return pltpu.make_async_remote_copy(
            src_ref=ref, dst_ref=ref, send_sem=isib_send.at[o], recv_sem=isib_recv.at[o],
            device_id=sibling, device_id_type=MESH,
        )

    has_tiles = z >= c
    relays = has_tiles & (z + 1 < planes)
    gives = (z > c) | ((z == c) & (k == 0))
    takes = (z > c) | ((z == c) & (k == 1))

    own = pl.ds(pl.multiple_of(c * piece, piece), piece)
    tiles[slot, own, :] = panel_ref[...]
    fold[pl.ds(pl.multiple_of(row * fold_rows, fold_rows), fold_rows), :] = fold_ref[...]
    inv_t[pl.ds(pl.multiple_of(c * inv_cols, inv_cols), inv_cols), :] = inv_ref[...].T

    pl.semaphore_wait(barrier, planes + groups - 1)

    def chain(j):
        for h in range(chunks):
            @pl.when(z > c)
            def _():
                up_copy(j, h).wait_recv()

            @pl.when((z == c) & (c != j))
            def _():
                rb_arrival(j, h).wait_recv()

            @pl.when(relays)
            def _():
                up_copy(j, h).start()

            @pl.when(gives)
            def _():
                sib_copy(k, j, h).start()

    for h in range(chunks):
        for o in range(1, groups):
            rb_copy(o, h).start()
    fsib_copy(0, k).start()
    for o in range(1, planes):
        fold_copy(o).start()
    for o in range(1, groups):
        inv_copy(o).start()

    per = max(1, min(groups, 256 // piece))
    halfway = groups // 2

    def products(first, last):
        size = (last - first) * piece
        for which in range(2):
            tile = k if which == 0 else 1 - k
            active = has_tiles if which == 0 else takes

            @pl.when(active)
            def _():
                if which == 1:
                    for j in range(first, last):
                        for h in range(chunks):
                            sib_copy(1 - k, j, h).wait_recv()
                part = split(tiles[tile, first * piece : last * piece, :])
                at = pl.ds(pl.multiple_of(tile * (groups * piece) + first * piece, size), size)
                update_ref[:, at] = dot3((q_hi[...], q_lo[...]), part, NT)

    for j in range(halfway // 2):
        chain(j)
    for o in range(1, planes):
        fold_arrival(o).wait_recv()
        fsib_copy(o, k).start()
    for o in range(1, groups):
        inv_arrival(o).wait_recv()
        isib_copy(o, k).start()
    for j in range(halfway // 2, halfway):
        chain(j)
    for o in range(1, groups):
        isib_copy(o, 1 - k).wait_recv()
    inverse = split(inv_t[...])
    g_hi[...], g_lo[...] = split(dot3(inverse, inverse, NT))
    for j in range(halfway, halfway + halfway // 2):
        chain(j)
    for j in range(groups):
        @pl.when((z != c) & (c != j))
        def _():
            for h in range(chunks):
                rb_arrival(j, h).wait_recv()
    for j in range(halfway + halfway // 2, groups):
        @pl.when((z == c))
        def _():
            chain(j)
    q_hi[...], q_lo[...] = split(dot3(split(tiles[slot]), (g_hi[...], g_lo[...]), NN))
    for o in range(planes):
        fsib_copy(o, 1 - k).wait_recv()
    corr_ref[...] = dot3((q_hi[...], q_lo[...]), split(fold[...]), NN)
    done = halfway + halfway // 2
    ready = (done // per) * per
    for first in range(0, ready, per):
        products(first, first + per)
    for j in range(done, groups):
        @pl.when(z > c)
        def _():
            chain(j)
    for first in range(ready, groups, per):
        products(first, min(first + per, groups))

    for h in range(chunks):
        for o in range(1, groups):
            rb_copy(o, h).wait_send()
    for o in range(1, planes):
        fold_copy(o).wait_send()
    for o in range(planes):
        fsib_copy(o, k).wait_send()
    for o in range(1, groups):
        inv_copy(o).wait_send()
        isib_copy(o, k).wait_send()

    @pl.when(relays)
    def _():
        for j in range(groups):
            for h in range(chunks):
                up_copy(j, h).wait_send()

    @pl.when(gives)
    def _():
        for j in range(groups):
            for h in range(chunks):
                sib_copy(k, j, h).wait_send()


def solution(mesh):
    rows_axis = mesh.shape["row"]
    groups = mesh.shape["col"]
    planes = rows_axis // 2
    chunks = 2

    def on_device(trailing, panel, inv_factor, later_series, fold_series, fold_len):
        rows_here, cols_here = trailing.shape
        piece, width = panel.shape
        series = fold_series.shape[1]
        assert rows_axis % 2 == 0 and cols_here == 2 * rows_here and groups <= planes
        dma = pltpu.SemaphoreType.DMA
        vmem = pl.BlockSpec(memory_space=pltpu.VMEM)
        update, corr = pl.pallas_call(
            functools.partial(kernel, planes, groups, chunks),
            out_shape=(
                jax.ShapeDtypeStruct((rows_here, cols_here), F32),
                jax.ShapeDtypeStruct((rows_here, series), F32),
            ),
            in_specs=[vmem] * 3,
            out_specs=(vmem, vmem),
            scratch_shapes=[
                pltpu.VMEM((3, rows_here, width), F32),
                pltpu.VMEM((width, width), F32),
                pltpu.VMEM((width, series), F32),
                pltpu.VMEM((rows_here, width), BF16),
                pltpu.VMEM((rows_here, width), BF16),
                pltpu.VMEM((width, width), BF16),
                pltpu.VMEM((width, width), BF16),
                dma((groups, chunks)), dma((groups, chunks)),
                dma((groups, chunks)), dma((groups, chunks)),
                dma((groups, chunks)), dma((groups, chunks)),
                dma((planes,)), dma((planes,)), dma((planes,)), dma((planes,)),
                dma((groups,)), dma((groups,)), dma((groups,)), dma((groups,)),
            ],
            compiler_params=pltpu.CompilerParams(
                collective_id=0, has_side_effects=True, vmem_limit_bytes=40 * 1024 * 1024
            ),
        )(panel, inv_factor, fold_series)
        row_pos = lax.axis_index("row")
        col_pos = lax.axis_index("col")
        col_tile = (col_pos * cols_here + jnp.arange(cols_here, dtype=jnp.int32)) // rows_here
        lower = col_tile <= row_pos
        new_trailing = jnp.where(lower[None, :], trailing - update, trailing)
        active = row_pos < fold_len
        new_series = jnp.where(active[None, :], later_series - corr, later_series)
        return (new_trailing, new_series)

    in_specs = (
        P("row", "col"),
        P(("row", "col"), None),
        P(None, "col"),
        P("row", "col"),
        P("row", "col"),
        P("col"),
    )
    out_specs = (P("row", "col"), P("row", "col"))
    return jax.shard_map(
        on_device, mesh=mesh, in_specs=in_specs, out_specs=out_specs, check_vma=False
    )
```

```python
import functools

import jax
import jax.numpy as jnp
from jax import lax
from jax.experimental import pallas as pl
from jax.experimental.pallas import tpu as pltpu
from jax.sharding import PartitionSpec as P

MESH = pl.DeviceIdType.MESH
F32 = jnp.float32
BF16 = jnp.bfloat16
NT = (((1,), (1,)), ((), ()))
NN = (((1,), (0,)), ((), ()))


def split(x):
    high = x.astype(BF16)
    return high, (x - high.astype(F32)).astype(BF16)


def dot3(a, b, dims):
    dot = functools.partial(lax.dot_general, dimension_numbers=dims, preferred_element_type=F32)
    return dot(a[0], b[0]) + (dot(a[0], b[1]) + dot(a[1], b[0]))


def kernel(
    planes, groups, chunks,
    trailing_ref, panel_ref, inv_ref, later_ref, fold_ref, len_ref,
    out_ref, series_ref,
    tiles, inv_in, inv_t, fold, lens, q_hi, q_lo, g_hi, g_lo, local,
    rb_send, rb_recv, up_send, up_recv, sib_send, sib_recv,
    fold_send, fold_recv, fsib_send, fsib_recv,
    inv_send, inv_recv, isib_send, isib_recv,
):
    row = lax.axis_index("row")
    c = lax.axis_index("col")
    z = row // 2
    k = row % 2
    piece = panel_ref.shape[0]
    step = piece // chunks
    width = panel_ref.shape[1]
    fold_rows = fold_ref.shape[0]
    inv_cols = inv_ref.shape[1]
    half = inv_cols // 2
    sibling = (2 * z + (1 - k), c)

    barrier = pltpu.get_barrier_semaphore()
    pl.semaphore_signal(barrier, inc=1, device_id=sibling, device_id_type=MESH)
    for o in range(1, planes):
        pl.semaphore_signal(
            barrier, inc=1, device_id=(2 * ((z + o) % planes) + k, c), device_id_type=MESH
        )
    for o in range(1, groups):
        pl.semaphore_signal(
            barrier, inc=1, device_id=(row, (c + o) % groups), device_id_type=MESH
        )

    def slot_of(col):
        return jnp.where(col == z, k, 2)

    slot = slot_of(c)

    def rows_of(j, h):
        return pl.ds(pl.multiple_of(j * piece + h * step, step), step)

    def rb_copy(o, h):
        target = (c + o) % groups
        return pltpu.make_async_remote_copy(
            src_ref=tiles.at[slot, rows_of(c, h)],
            dst_ref=tiles.at[slot_of(target), rows_of(c, h)],
            send_sem=rb_send.at[o, h],
            recv_sem=rb_recv.at[c, h],
            device_id=(row, target),
            device_id_type=MESH,
        )

    def rb_arrival(j, h):
        return pltpu.make_async_remote_copy(
            src_ref=tiles.at[slot, rows_of(j, h)],
            dst_ref=tiles.at[slot, rows_of(j, h)],
            send_sem=rb_send.at[0, h],
            recv_sem=rb_recv.at[j, h],
            device_id=sibling,
            device_id_type=MESH,
        )

    def up_copy(j, h):
        return pltpu.make_async_remote_copy(
            src_ref=tiles.at[k, rows_of(j, h)],
            dst_ref=tiles.at[k, rows_of(j, h)],
            send_sem=up_send.at[j, h],
            recv_sem=up_recv.at[j, h],
            device_id=(jnp.minimum(row + 2, 2 * planes - 2 + k), c),
            device_id_type=MESH,
        )

    def sib_copy(tile, j, h):
        return pltpu.make_async_remote_copy(
            src_ref=tiles.at[tile, rows_of(j, h)],
            dst_ref=tiles.at[tile, rows_of(j, h)],
            send_sem=sib_send.at[j, h],
            recv_sem=sib_recv.at[j, h],
            device_id=sibling,
            device_id_type=MESH,
        )

    def fold_at(plane, core):
        return fold.at[pl.ds(pl.multiple_of((2 * plane + core) * fold_rows, fold_rows), fold_rows)]

    def fold_copy(o):
        target = (z + o) % planes
        return pltpu.make_async_remote_copy(
            src_ref=fold_at(z, k),
            dst_ref=fold_at(z, k),
            send_sem=fold_send.at[o],
            recv_sem=fold_recv.at[planes - o],
            device_id=(2 * target + k, c),
            device_id_type=MESH,
        )

    def fold_arrival(o):
        ref = fold_at((z + o) % planes, k)
        return pltpu.make_async_remote_copy(
            src_ref=ref, dst_ref=ref, send_sem=fold_send.at[0], recv_sem=fold_recv.at[o],
            device_id=sibling, device_id_type=MESH,
        )

    def fsib_copy(o, core):
        ref = fold_at((z + o) % planes, core)
        return pltpu.make_async_remote_copy(
            src_ref=ref, dst_ref=ref, send_sem=fsib_send.at[o], recv_sem=fsib_recv.at[o],
            device_id=sibling, device_id_type=MESH,
        )

    def inv_at(col, core):
        return inv_t.at[pl.ds(pl.multiple_of(col * inv_cols + core * half, half), half)]

    def inv_copy(o):
        return pltpu.make_async_remote_copy(
            src_ref=inv_at(c, k),
            dst_ref=inv_at(c, k),
            send_sem=inv_send.at[o],
            recv_sem=inv_recv.at[groups - o],
            device_id=(row, (c + o) % groups),
            device_id_type=MESH,
        )

    def inv_arrival(o):
        ref = inv_at((c + o) % groups, k)
        return pltpu.make_async_remote_copy(
            src_ref=ref, dst_ref=ref, send_sem=inv_send.at[0], recv_sem=inv_recv.at[o],
            device_id=sibling, device_id_type=MESH,
        )

    def isib_copy(o, core):
        ref = inv_at((c + o) % groups, core)
        return pltpu.make_async_remote_copy(
            src_ref=ref, dst_ref=ref, send_sem=isib_send.at[o], recv_sem=isib_recv.at[o],
            device_id=sibling, device_id_type=MESH,
        )

    has_tiles = z >= c
    relays = has_tiles & (z + 1 < planes)
    gives = (z > c) | ((z == c) & (k == 0))
    takes = (z > c) | ((z == c) & (k == 1))

    own = pl.ds(pl.multiple_of(c * piece, piece), piece)
    fetches = [
        pltpu.make_async_copy(src, dst, local.at[n])
        for n, (src, dst) in enumerate((
            (panel_ref, tiles.at[slot, own]),
            (fold_ref, fold_at(z, k)),
            (inv_ref, inv_in),
            (trailing_ref, out_ref),
            (later_ref, series_ref),
            (len_ref, lens),
        ))
    ]
    for fetch in fetches:
        fetch.start()
    pl.semaphore_wait(barrier, planes + groups - 1)

    def chain(j):
        for h in range(chunks):
            @pl.when(z > c)
            def _():
                up_copy(j, h).wait_recv()

            @pl.when((z == c) & (c != j))
            def _():
                rb_arrival(j, h).wait_recv()

            @pl.when(relays)
            def _():
                up_copy(j, h).start()

            @pl.when(gives)
            def _():
                sib_copy(k, j, h).start()

    ordered = (z < groups) & (z != c) & (z + 1 < planes)

    def is_first(o):
        return ordered & ((c + o) % groups == z)

    fetches[0].wait()
    for o in range(1, groups):
        @pl.when(is_first(o))
        def _():
            for h in range(chunks):
                rb_copy(o, h).start()

    fetches[1].wait()
    fsib_copy(0, k).start()
    for o in range(1, planes):
        fold_copy(o).start()
    fetches[2].wait()
    inv_t[pl.ds(pl.multiple_of(c * inv_cols, inv_cols), inv_cols), :] = inv_in[...].T

    def send_rest():
        for o in range(1, groups):
            @pl.when(is_first(o))
            def _():
                for h in range(chunks):
                    rb_copy(o, h).wait_send()
        for o in range(1, groups):
            @pl.when(jnp.logical_not(is_first(o)))
            def _():
                for h in range(chunks):
                    rb_copy(o, h).start()
        for o in range(1, groups):
            inv_copy(o).start()

    early = (z <= c) | (z + 1 >= planes)

    @pl.when(early)
    def _():
        send_rest()

    per = max(1, min(groups, 256 // piece))
    halfway = groups // 2

    def products(first, last):
        size = (last - first) * piece
        for which in range(2):
            tile = k if which == 0 else 1 - k
            active = has_tiles if which == 0 else takes

            @pl.when(active)
            def _():
                if which == 1:
                    for j in range(first, last):
                        for h in range(chunks):
                            sib_copy(1 - k, j, h).wait_recv()
                part = split(tiles[tile, first * piece : last * piece, :])
                at = pl.ds(pl.multiple_of(tile * (groups * piece) + first * piece, size), size)
                out_ref[:, at] = out_ref[:, at] - dot3((q_hi[...], q_lo[...]), part, NT)

    for j in range(halfway // 2):
        chain(j)

    @pl.when(jnp.logical_not(early))
    def _():
        send_rest()

    for o in range(1, planes):
        fold_arrival(o).wait_recv()
        fsib_copy(o, k).start()
    for o in range(1, groups):
        inv_arrival(o).wait_recv()
        isib_copy(o, k).start()
    for j in range(halfway // 2, halfway):
        chain(j)
    for o in range(1, groups):
        isib_copy(o, 1 - k).wait_recv()
    inverse = split(inv_t[...])
    g_hi[...], g_lo[...] = split(dot3(inverse, inverse, NT))
    for j in range(halfway, halfway + halfway // 2):
        chain(j)
    for j in range(groups):
        @pl.when((z != c) & (c != j))
        def _():
            for h in range(chunks):
                rb_arrival(j, h).wait_recv()
    for j in range(halfway + halfway // 2, groups):
        @pl.when((z == c))
        def _():
            chain(j)
    q_hi[...], q_lo[...] = split(dot3(split(tiles[slot]), (g_hi[...], g_lo[...]), NN))
    for o in range(planes):
        fsib_copy(o, 1 - k).wait_recv()
    correction = dot3((q_hi[...], q_lo[...]), split(fold[...]), NN)
    for fetch in fetches[3:]:
        fetch.wait()
    later = series_ref[...]
    series_ref[...] = jnp.where(row < lens[...], later - correction, later)
    done = halfway + halfway // 2
    ready = (done // per) * per
    for first in range(0, ready, per):
        products(first, first + per)
    for j in range(done, groups):
        @pl.when(z > c)
        def _():
            chain(j)
    for first in range(ready, groups, per):
        products(first, min(first + per, groups))

    for o in range(1, groups):
        @pl.when(jnp.logical_not(is_first(o)))
        def _():
            for h in range(chunks):
                rb_copy(o, h).wait_send()
    for o in range(1, planes):
        fold_copy(o).wait_send()
    for o in range(planes):
        fsib_copy(o, k).wait_send()
    for o in range(1, groups):
        inv_copy(o).wait_send()
        isib_copy(o, k).wait_send()

    @pl.when(relays)
    def _():
        for j in range(groups):
            for h in range(chunks):
                up_copy(j, h).wait_send()

    @pl.when(gives)
    def _():
        for j in range(groups):
            for h in range(chunks):
                sib_copy(k, j, h).wait_send()


def solution(mesh):
    rows_axis = mesh.shape["row"]
    groups = mesh.shape["col"]
    planes = rows_axis // 2
    chunks = 4

    def on_device(trailing, panel, inv_factor, later_series, fold_series, fold_len):
        rows_here, cols_here = trailing.shape
        piece, width = panel.shape
        series = fold_series.shape[1]
        assert rows_axis % 2 == 0 and cols_here == 2 * rows_here and groups <= planes
        dma = pltpu.SemaphoreType.DMA
        vmem = pl.BlockSpec(memory_space=pltpu.VMEM)
        return pl.pallas_call(
            functools.partial(kernel, planes, groups, chunks),
            out_shape=(
                jax.ShapeDtypeStruct((rows_here, cols_here), F32),
                jax.ShapeDtypeStruct((rows_here, series), F32),
            ),
            in_specs=[pl.BlockSpec(memory_space=pltpu.HBM)] * 6,
            out_specs=(vmem, vmem),
            scratch_shapes=[
                pltpu.VMEM((3, rows_here, width), F32),
                pltpu.VMEM(inv_factor.shape, F32),
                pltpu.VMEM((width, width), F32),
                pltpu.VMEM((width, series), F32),
                pltpu.VMEM((1, series), jnp.int32),
                pltpu.VMEM((rows_here, width), BF16),
                pltpu.VMEM((rows_here, width), BF16),
                pltpu.VMEM((width, width), BF16),
                pltpu.VMEM((width, width), BF16),
                dma((6,)),
                dma((groups, chunks)), dma((groups, chunks)),
                dma((groups, chunks)), dma((groups, chunks)),
                dma((groups, chunks)), dma((groups, chunks)),
                dma((planes,)), dma((planes,)), dma((planes,)), dma((planes,)),
                dma((groups,)), dma((groups,)), dma((groups,)), dma((groups,)),
            ],
            compiler_params=pltpu.CompilerParams(
                collective_id=0, has_side_effects=True, vmem_limit_bytes=32 * 1024 * 1024
            ),
        )(trailing, panel, inv_factor, later_series, fold_series, fold_len.reshape(1, series))

    in_specs = (
        P("row", "col"),
        P(("row", "col"), None),
        P(None, "col"),
        P("row", "col"),
        P("row", "col"),
        P("col"),
    )
    out_specs = (P("row", "col"), P("row", "col"))
    return jax.shard_map(
        on_device, mesh=mesh, in_specs=in_specs, out_specs=out_specs, check_vma=False
    )
```

```python
import functools

import jax
import jax.numpy as jnp
from jax import lax
from jax.experimental import pallas as pl
from jax.experimental.pallas import tpu as pltpu
from jax.sharding import PartitionSpec as P

MESH = pl.DeviceIdType.MESH
F32 = jnp.float32
BF16 = jnp.bfloat16
NT = (((1,), (1,)), ((), ()))
NN = (((1,), (0,)), ((), ()))


def split(x):
    high = x.astype(BF16)
    return high, (x - high.astype(F32)).astype(BF16)


def dot3(a, b, dims):
    dot = functools.partial(lax.dot_general, dimension_numbers=dims, preferred_element_type=F32)
    return dot(a[0], b[0]) + (dot(a[0], b[1]) + dot(a[1], b[0]))


def kernel(
    planes, groups, chunks,
    trailing_ref, panel_ref, inv_ref, later_ref, fold_ref, len_ref,
    out_ref, series_ref,
    tiles, inv_in, inv_t, fold, lens, q_hi, q_lo, g_hi, g_lo, local,
    rb_send, rb_recv, up_send, up_recv, sib_send, sib_recv,
    fold_send, fold_recv, fsib_send, fsib_recv,
    inv_send, inv_recv, isib_send, isib_recv,
):
    row = lax.axis_index("row")
    c = lax.axis_index("col")
    z = row // 2
    k = row % 2
    piece = panel_ref.shape[0]
    step = piece // chunks
    width = panel_ref.shape[1]
    fold_rows = fold_ref.shape[0]
    inv_cols = inv_ref.shape[1]
    half = inv_cols // 2
    sibling = (2 * z + (1 - k), c)

    barrier = pltpu.get_barrier_semaphore()
    pl.semaphore_signal(barrier, inc=1, device_id=sibling, device_id_type=MESH)
    for o in range(1, planes):
        pl.semaphore_signal(
            barrier, inc=1, device_id=(2 * ((z + o) % planes) + k, c), device_id_type=MESH
        )
    for o in range(1, groups):
        pl.semaphore_signal(
            barrier, inc=1, device_id=(row, (c + o) % groups), device_id_type=MESH
        )

    def slot_of(col):
        return jnp.where(col == z, k, 2)

    slot = slot_of(c)

    def rows_of(j, h):
        return pl.ds(pl.multiple_of(j * piece + h * step, step), step)

    def rb_copy(o, h):
        target = (c + o) % groups
        return pltpu.make_async_remote_copy(
            src_ref=tiles.at[slot, rows_of(c, h)],
            dst_ref=tiles.at[slot_of(target), rows_of(c, h)],
            send_sem=rb_send.at[o, h],
            recv_sem=rb_recv.at[c, h],
            device_id=(row, target),
            device_id_type=MESH,
        )

    def rb_arrival(j, h):
        return pltpu.make_async_remote_copy(
            src_ref=tiles.at[slot, rows_of(j, h)],
            dst_ref=tiles.at[slot, rows_of(j, h)],
            send_sem=rb_send.at[0, h],
            recv_sem=rb_recv.at[j, h],
            device_id=sibling,
            device_id_type=MESH,
        )

    def up_copy(j, h):
        return pltpu.make_async_remote_copy(
            src_ref=tiles.at[k, rows_of(j, h)],
            dst_ref=tiles.at[k, rows_of(j, h)],
            send_sem=up_send.at[j, h],
            recv_sem=up_recv.at[j, h],
            device_id=(jnp.minimum(row + 2, 2 * planes - 2 + k), c),
            device_id_type=MESH,
        )

    def sib_copy(tile, j, h):
        return pltpu.make_async_remote_copy(
            src_ref=tiles.at[tile, rows_of(j, h)],
            dst_ref=tiles.at[tile, rows_of(j, h)],
            send_sem=sib_send.at[j, h],
            recv_sem=sib_recv.at[j, h],
            device_id=sibling,
            device_id_type=MESH,
        )

    def fold_at(plane, core):
        return fold.at[pl.ds(pl.multiple_of((2 * plane + core) * fold_rows, fold_rows), fold_rows)]

    def fold_copy(o):
        target = (z + o) % planes
        return pltpu.make_async_remote_copy(
            src_ref=fold_at(z, k),
            dst_ref=fold_at(z, k),
            send_sem=fold_send.at[o],
            recv_sem=fold_recv.at[planes - o],
            device_id=(2 * target + k, c),
            device_id_type=MESH,
        )

    def fold_arrival(o):
        ref = fold_at((z + o) % planes, k)
        return pltpu.make_async_remote_copy(
            src_ref=ref, dst_ref=ref, send_sem=fold_send.at[0], recv_sem=fold_recv.at[o],
            device_id=sibling, device_id_type=MESH,
        )

    def fsib_copy(o, core):
        ref = fold_at((z + o) % planes, core)
        return pltpu.make_async_remote_copy(
            src_ref=ref, dst_ref=ref, send_sem=fsib_send.at[o], recv_sem=fsib_recv.at[o],
            device_id=sibling, device_id_type=MESH,
        )

    def inv_at(col, core):
        return inv_t.at[pl.ds(pl.multiple_of(col * inv_cols + core * half, half), half)]

    def inv_copy(o):
        return pltpu.make_async_remote_copy(
            src_ref=inv_at(c, k),
            dst_ref=inv_at(c, k),
            send_sem=inv_send.at[o],
            recv_sem=inv_recv.at[groups - o],
            device_id=(row, (c + o) % groups),
            device_id_type=MESH,
        )

    def inv_arrival(o):
        ref = inv_at((c + o) % groups, k)
        return pltpu.make_async_remote_copy(
            src_ref=ref, dst_ref=ref, send_sem=inv_send.at[0], recv_sem=inv_recv.at[o],
            device_id=sibling, device_id_type=MESH,
        )

    def isib_copy(o, core):
        ref = inv_at((c + o) % groups, core)
        return pltpu.make_async_remote_copy(
            src_ref=ref, dst_ref=ref, send_sem=isib_send.at[o], recv_sem=isib_recv.at[o],
            device_id=sibling, device_id_type=MESH,
        )

    has_tiles = z >= c
    relays = has_tiles & (z + 1 < planes)
    gives = (z > c) | ((z == c) & (k == 0))
    takes = (z > c) | ((z == c) & (k == 1))

    own = pl.ds(pl.multiple_of(c * piece, piece), piece)
    fetches = [
        pltpu.make_async_copy(src, dst, local.at[n])
        for n, (src, dst) in enumerate((
            (panel_ref, tiles.at[slot, own]),
            (fold_ref, fold_at(z, k)),
            (inv_ref, inv_in),
            (trailing_ref, out_ref),
            (later_ref, series_ref),
            (len_ref, lens),
        ))
    ]
    for fetch in fetches:
        fetch.start()
    pl.semaphore_wait(barrier, planes + groups - 1)

    def chain(j):
        for h in range(chunks):
            @pl.when(z > c)
            def _():
                up_copy(j, h).wait_recv()

            @pl.when((z == c) & (c != j))
            def _():
                rb_arrival(j, h).wait_recv()

            @pl.when(relays)
            def _():
                up_copy(j, h).start()

            @pl.when(gives)
            def _():
                sib_copy(k, j, h).start()

    ordered = (z < groups) & (z != c) & (z + 1 < planes)

    def is_first(o):
        return ordered & ((c + o) % groups == z)

    fetches[0].wait()
    for o in range(1, groups):
        @pl.when(is_first(o))
        def _():
            for h in range(chunks):
                rb_copy(o, h).start()

    fetches[1].wait()
    fsib_copy(0, k).start()
    for o in range(1, planes):
        fold_copy(o).start()
    fetches[2].wait()
    inv_t[pl.ds(pl.multiple_of(c * inv_cols, inv_cols), inv_cols), :] = inv_in[...].T

    for h in range(chunks):
        for o in range(1, groups):
            @pl.when(jnp.logical_not(is_first(o)))
            def _():
                rb_copy(o, h).start()
    for o in range(1, groups):
        @pl.when(jnp.logical_not(is_first(o)))
        def _():
            inv_copy(o).start()

    def send_last():
        for o in range(1, groups):
            @pl.when(is_first(o))
            def _():
                for h in range(chunks):
                    rb_copy(o, h).wait_send()
                inv_copy(o).start()

    below = z > c

    def relay(first, last):
        @pl.when(below)
        def _():
            for j in range(first, last):
                chain(j)

    @pl.when(z == c)
    def _():
        for j in range(groups):
            chain(j)

    @pl.when(jnp.logical_not(below))
    def _():
        send_last()

    per = max(1, min(groups, 256 // piece))
    halfway = groups // 2

    def products(first, last):
        size = (last - first) * piece
        for which in range(2):
            tile = k if which == 0 else 1 - k
            active = has_tiles if which == 0 else takes

            @pl.when(active)
            def _():
                if which == 1:
                    for j in range(first, last):
                        for h in range(chunks):
                            sib_copy(1 - k, j, h).wait_recv()
                part = split(tiles[tile, first * piece : last * piece, :])
                at = pl.ds(pl.multiple_of(tile * (groups * piece) + first * piece, size), size)
                out_ref[:, at] = out_ref[:, at] - dot3((q_hi[...], q_lo[...]), part, NT)

    relay(0, halfway // 2)

    @pl.when(below)
    def _():
        send_last()

    for o in range(1, planes):
        fold_arrival(o).wait_recv()
        fsib_copy(o, k).start()
    relay(halfway // 2, halfway)
    for o in range(1, groups):
        inv_arrival(o).wait_recv()
        isib_copy(o, k).start()
    for o in range(1, groups):
        isib_copy(o, 1 - k).wait_recv()
    inverse = split(inv_t[...])
    g_hi[...], g_lo[...] = split(dot3(inverse, inverse, NT))
    relay(halfway, halfway + halfway // 2)
    for j in range(groups):
        @pl.when((z != c) & (c != j))
        def _():
            for h in range(chunks):
                rb_arrival(j, h).wait_recv()
    q_hi[...], q_lo[...] = split(dot3(split(tiles[slot]), (g_hi[...], g_lo[...]), NN))
    for o in range(planes):
        fsib_copy(o, 1 - k).wait_recv()
    correction = dot3((q_hi[...], q_lo[...]), split(fold[...]), NN)
    for fetch in fetches[3:]:
        fetch.wait()
    later = series_ref[...]
    series_ref[...] = jnp.where(row < lens[...], later - correction, later)
    done = halfway + halfway // 2
    ready = (done // per) * per
    for first in range(0, ready, per):
        products(first, first + per)
    relay(done, groups)
    for first in range(ready, groups, per):
        products(first, min(first + per, groups))

    for o in range(1, groups):
        @pl.when(jnp.logical_not(is_first(o)))
        def _():
            for h in range(chunks):
                rb_copy(o, h).wait_send()
    for o in range(1, planes):
        fold_copy(o).wait_send()
    for o in range(planes):
        fsib_copy(o, k).wait_send()
    for o in range(1, groups):
        inv_copy(o).wait_send()
        isib_copy(o, k).wait_send()

    @pl.when(relays)
    def _():
        for j in range(groups):
            for h in range(chunks):
                up_copy(j, h).wait_send()

    @pl.when(gives)
    def _():
        for j in range(groups):
            for h in range(chunks):
                sib_copy(k, j, h).wait_send()


def solution(mesh):
    rows_axis = mesh.shape["row"]
    groups = mesh.shape["col"]
    planes = rows_axis // 2
    chunks = 4

    def on_device(trailing, panel, inv_factor, later_series, fold_series, fold_len):
        rows_here, cols_here = trailing.shape
        piece, width = panel.shape
        series = fold_series.shape[1]
        assert rows_axis % 2 == 0 and cols_here == 2 * rows_here and groups <= planes
        dma = pltpu.SemaphoreType.DMA
        vmem = pl.BlockSpec(memory_space=pltpu.VMEM)
        return pl.pallas_call(
            functools.partial(kernel, planes, groups, chunks),
            out_shape=(
                jax.ShapeDtypeStruct((rows_here, cols_here), F32),
                jax.ShapeDtypeStruct((rows_here, series), F32),
            ),
            in_specs=[pl.BlockSpec(memory_space=pltpu.HBM)] * 6,
            out_specs=(vmem, vmem),
            scratch_shapes=[
                pltpu.VMEM((3, rows_here, width), F32),
                pltpu.VMEM(inv_factor.shape, F32),
                pltpu.VMEM((width, width), F32),
                pltpu.VMEM((width, series), F32),
                pltpu.VMEM((1, series), jnp.int32),
                pltpu.VMEM((rows_here, width), BF16),
                pltpu.VMEM((rows_here, width), BF16),
                pltpu.VMEM((width, width), BF16),
                pltpu.VMEM((width, width), BF16),
                dma((6,)),
                dma((groups, chunks)), dma((groups, chunks)),
                dma((groups, chunks)), dma((groups, chunks)),
                dma((groups, chunks)), dma((groups, chunks)),
                dma((planes,)), dma((planes,)), dma((planes,)), dma((planes,)),
                dma((groups,)), dma((groups,)), dma((groups,)), dma((groups,)),
            ],
            compiler_params=pltpu.CompilerParams(
                collective_id=0, has_side_effects=True, vmem_limit_bytes=56 * 1024 * 1024
            ),
        )(trailing, panel, inv_factor, later_series, fold_series, fold_len.reshape(1, series))

    in_specs = (
        P("row", "col"),
        P(("row", "col"), None),
        P(None, "col"),
        P("row", "col"),
        P("row", "col"),
        P("col"),
    )
    out_specs = (P("row", "col"), P("row", "col"))
    return jax.shard_map(
        on_device, mesh=mesh, in_specs=in_specs, out_specs=out_specs, check_vma=False
    )
```

```python
import functools

import jax
import jax.numpy as jnp
from jax import lax
from jax.experimental import pallas as pl
from jax.experimental.pallas import tpu as pltpu
from jax.sharding import PartitionSpec as P

MESH = pl.DeviceIdType.MESH
F32 = jnp.float32
BF16 = jnp.bfloat16
NT = (((1,), (1,)), ((), ()))
NN = (((1,), (0,)), ((), ()))


def split(x):
    high = x.astype(BF16)
    return high, (x - high.astype(F32)).astype(BF16)


def dot3(a, b, dims):
    dot = functools.partial(lax.dot_general, dimension_numbers=dims, preferred_element_type=F32)
    return dot(a[0], b[0]) + (dot(a[0], b[1]) + dot(a[1], b[0]))


def kernel(
    planes, groups, chunks,
    trailing_ref, panel_ref, inv_ref, later_ref, fold_ref, len_ref,
    out_ref, series_ref,
    tiles, inv_in, inv_t, fold, lens, q_hi, q_lo, g_hi, g_lo, local,
    rb_send, rb_recv, up_send, up_recv, sib_send, sib_recv,
    fold_send, fold_recv, fsib_send, fsib_recv,
    inv_send, inv_recv, isib_send, isib_recv,
):
    row = lax.axis_index("row")
    c = lax.axis_index("col")
    z = row // 2
    k = row % 2
    piece = panel_ref.shape[0]
    step = piece // chunks
    width = panel_ref.shape[1]
    fold_rows = fold_ref.shape[0]
    inv_cols = inv_ref.shape[1]
    half = inv_cols // 2
    sibling = (2 * z + (1 - k), c)

    barrier = pltpu.get_barrier_semaphore()
    pl.semaphore_signal(barrier, inc=1, device_id=sibling, device_id_type=MESH)
    for o in range(1, planes):
        pl.semaphore_signal(
            barrier, inc=1, device_id=(2 * ((z + o) % planes) + k, c), device_id_type=MESH
        )
    for o in range(1, groups):
        pl.semaphore_signal(
            barrier, inc=1, device_id=(row, (c + o) % groups), device_id_type=MESH
        )

    def slot_of(col):
        return jnp.where(col == z, k, 2)

    slot = slot_of(c)

    def rows_of(j, h):
        return pl.ds(pl.multiple_of(j * piece + h * step, step), step)

    def rb_copy(o, h):
        target = (c + o) % groups
        return pltpu.make_async_remote_copy(
            src_ref=tiles.at[slot, rows_of(c, h)],
            dst_ref=tiles.at[slot_of(target), rows_of(c, h)],
            send_sem=rb_send.at[o, h],
            recv_sem=rb_recv.at[c, h],
            device_id=(row, target),
            device_id_type=MESH,
        )

    def rb_arrival(j, h):
        return pltpu.make_async_remote_copy(
            src_ref=tiles.at[slot, rows_of(j, h)],
            dst_ref=tiles.at[slot, rows_of(j, h)],
            send_sem=rb_send.at[0, h],
            recv_sem=rb_recv.at[j, h],
            device_id=sibling,
            device_id_type=MESH,
        )

    def up_copy(j, h):
        return pltpu.make_async_remote_copy(
            src_ref=tiles.at[k, rows_of(j, h)],
            dst_ref=tiles.at[k, rows_of(j, h)],
            send_sem=up_send.at[j, h],
            recv_sem=up_recv.at[j, h],
            device_id=(jnp.minimum(row + 2, 2 * planes - 2 + k), c),
            device_id_type=MESH,
        )

    def sib_copy(tile, j, h):
        return pltpu.make_async_remote_copy(
            src_ref=tiles.at[tile, rows_of(j, h)],
            dst_ref=tiles.at[tile, rows_of(j, h)],
            send_sem=sib_send.at[j, h],
            recv_sem=sib_recv.at[j, h],
            device_id=sibling,
            device_id_type=MESH,
        )

    def fold_at(plane, core):
        return fold.at[pl.ds(pl.multiple_of((2 * plane + core) * fold_rows, fold_rows), fold_rows)]

    def fold_copy(o):
        target = (z + o) % planes
        return pltpu.make_async_remote_copy(
            src_ref=fold_at(z, k),
            dst_ref=fold_at(z, k),
            send_sem=fold_send.at[o],
            recv_sem=fold_recv.at[planes - o],
            device_id=(2 * target + k, c),
            device_id_type=MESH,
        )

    def fold_arrival(o):
        ref = fold_at((z + o) % planes, k)
        return pltpu.make_async_remote_copy(
            src_ref=ref, dst_ref=ref, send_sem=fold_send.at[0], recv_sem=fold_recv.at[o],
            device_id=sibling, device_id_type=MESH,
        )

    def fsib_copy(o, core):
        ref = fold_at((z + o) % planes, core)
        return pltpu.make_async_remote_copy(
            src_ref=ref, dst_ref=ref, send_sem=fsib_send.at[o], recv_sem=fsib_recv.at[o],
            device_id=sibling, device_id_type=MESH,
        )

    def inv_at(col, core):
        return inv_t.at[pl.ds(pl.multiple_of(col * inv_cols + core * half, half), half)]

    def inv_copy(o):
        return pltpu.make_async_remote_copy(
            src_ref=inv_at(c, k),
            dst_ref=inv_at(c, k),
            send_sem=inv_send.at[o],
            recv_sem=inv_recv.at[groups - o],
            device_id=(row, (c + o) % groups),
            device_id_type=MESH,
        )

    def inv_arrival(o):
        ref = inv_at((c + o) % groups, k)
        return pltpu.make_async_remote_copy(
            src_ref=ref, dst_ref=ref, send_sem=inv_send.at[0], recv_sem=inv_recv.at[o],
            device_id=sibling, device_id_type=MESH,
        )

    def isib_copy(o, core):
        ref = inv_at((c + o) % groups, core)
        return pltpu.make_async_remote_copy(
            src_ref=ref, dst_ref=ref, send_sem=isib_send.at[o], recv_sem=isib_recv.at[o],
            device_id=sibling, device_id_type=MESH,
        )

    has_tiles = z >= c
    relays = has_tiles & (z + 1 < planes)
    gives = (z > c) | ((z == c) & (k == 0))
    takes = (z > c) | ((z == c) & (k == 1))

    own = pl.ds(pl.multiple_of(c * piece, piece), piece)
    fetches = [
        pltpu.make_async_copy(src, dst, local.at[n])
        for n, (src, dst) in enumerate((
            (panel_ref, tiles.at[slot, own]),
            (fold_ref, fold_at(z, k)),
            (inv_ref, inv_in),
            (trailing_ref, out_ref),
            (later_ref, series_ref),
            (len_ref, lens),
        ))
    ]
    for fetch in fetches:
        fetch.start()
    pl.semaphore_wait(barrier, planes + groups - 1)

    def chain(j):
        for h in range(chunks):
            @pl.when(z > c)
            def _():
                up_copy(j, h).wait_recv()

            @pl.when((z == c) & (c != j))
            def _():
                rb_arrival(j, h).wait_recv()

            @pl.when(relays)
            def _():
                up_copy(j, h).start()

            @pl.when(gives)
            def _():
                sib_copy(k, j, h).start()

    ordered = (z < groups) & (z != c) & (z + 1 < planes)

    def is_first(o):
        return ordered & ((c + o) % groups == z)

    fetches[0].wait()
    for o in range(1, groups):
        @pl.when(is_first(o))
        def _():
            for h in range(chunks):
                rb_copy(o, h).start()

    fetches[1].wait()
    fsib_copy(0, k).start()
    for o in range(1, planes):
        fold_copy(o).start()
    fetches[2].wait()
    inv_t[pl.ds(pl.multiple_of(c * inv_cols, inv_cols), inv_cols), :] = inv_in[...].T

    for h in range(chunks):
        for o in range(1, groups):
            @pl.when(jnp.logical_not(is_first(o)))
            def _():
                rb_copy(o, h).start()
    for o in range(1, groups):
        @pl.when(jnp.logical_not(is_first(o)))
        def _():
            inv_copy(o).start()

    def send_last():
        for o in range(1, groups):
            @pl.when(is_first(o))
            def _():
                for h in range(chunks):
                    rb_copy(o, h).wait_send()
                inv_copy(o).start()

    below = z > c

    top = below & (z + 1 >= planes)

    def relay(first, last, where=below):
        @pl.when(where)
        def _():
            for j in range(first, last):
                chain(j)

    @pl.when(z == c)
    def _():
        for j in range(groups):
            chain(j)

    @pl.when(jnp.logical_not(below))
    def _():
        send_last()

    per = max(1, min(groups, 256 // piece))
    halfway = groups // 2

    def products(first, last):
        size = (last - first) * piece
        for which in range(2):
            tile = k if which == 0 else 1 - k
            active = has_tiles if which == 0 else takes

            @pl.when(active)
            def _():
                if which == 1:
                    for j in range(first, last):
                        for h in range(chunks):
                            sib_copy(1 - k, j, h).wait_recv()
                part = split(tiles[tile, first * piece : last * piece, :])
                at = pl.ds(pl.multiple_of(tile * (groups * piece) + first * piece, size), size)
                out_ref[:, at] = out_ref[:, at] - dot3((q_hi[...], q_lo[...]), part, NT)

    relay(0, halfway // 2)

    @pl.when(below)
    def _():
        send_last()

    for o in range(1, planes):
        fold_arrival(o).wait_recv()
        fsib_copy(o, k).start()
    relay(halfway // 2, halfway)
    relay(halfway, groups, below & relays)
    for o in range(1, groups):
        inv_arrival(o).wait_recv()
        isib_copy(o, k).start()
    for o in range(1, groups):
        isib_copy(o, 1 - k).wait_recv()
    inverse = split(inv_t[...])
    g_hi[...], g_lo[...] = split(dot3(inverse, inverse, NT))
    relay(halfway, halfway + halfway // 2, top)
    for j in range(groups):
        @pl.when((z != c) & (c != j))
        def _():
            for h in range(chunks):
                rb_arrival(j, h).wait_recv()
    q_hi[...], q_lo[...] = split(dot3(split(tiles[slot]), (g_hi[...], g_lo[...]), NN))
    for o in range(planes):
        fsib_copy(o, 1 - k).wait_recv()
    correction = dot3((q_hi[...], q_lo[...]), split(fold[...]), NN)
    for fetch in fetches[3:]:
        fetch.wait()
    later = series_ref[...]
    series_ref[...] = jnp.where(row < lens[...], later - correction, later)
    done = halfway + halfway // 2
    ready = (done // per) * per
    for first in range(0, ready, per):
        products(first, first + per)
    relay(done, groups, top)
    for first in range(ready, groups, per):
        products(first, min(first + per, groups))

    for o in range(1, groups):
        @pl.when(jnp.logical_not(is_first(o)))
        def _():
            for h in range(chunks):
                rb_copy(o, h).wait_send()
    for o in range(1, planes):
        fold_copy(o).wait_send()
    for o in range(planes):
        fsib_copy(o, k).wait_send()
    for o in range(1, groups):
        inv_copy(o).wait_send()
        isib_copy(o, k).wait_send()

    @pl.when(relays)
    def _():
        for j in range(groups):
            for h in range(chunks):
                up_copy(j, h).wait_send()

    @pl.when(gives)
    def _():
        for j in range(groups):
            for h in range(chunks):
                sib_copy(k, j, h).wait_send()


def solution(mesh):
    rows_axis = mesh.shape["row"]
    groups = mesh.shape["col"]
    planes = rows_axis // 2
    chunks = 4

    def on_device(trailing, panel, inv_factor, later_series, fold_series, fold_len):
        rows_here, cols_here = trailing.shape
        piece, width = panel.shape
        series = fold_series.shape[1]
        assert rows_axis % 2 == 0 and cols_here == 2 * rows_here and groups <= planes
        dma = pltpu.SemaphoreType.DMA
        vmem = pl.BlockSpec(memory_space=pltpu.VMEM)
        return pl.pallas_call(
            functools.partial(kernel, planes, groups, chunks),
            out_shape=(
                jax.ShapeDtypeStruct((rows_here, cols_here), F32),
                jax.ShapeDtypeStruct((rows_here, series), F32),
            ),
            in_specs=[pl.BlockSpec(memory_space=pltpu.HBM)] * 6,
            out_specs=(vmem, vmem),
            scratch_shapes=[
                pltpu.VMEM((3, rows_here, width), F32),
                pltpu.VMEM(inv_factor.shape, F32),
                pltpu.VMEM((width, width), F32),
                pltpu.VMEM((width, series), F32),
                pltpu.VMEM((1, series), jnp.int32),
                pltpu.VMEM((rows_here, width), BF16),
                pltpu.VMEM((rows_here, width), BF16),
                pltpu.VMEM((width, width), BF16),
                pltpu.VMEM((width, width), BF16),
                dma((6,)),
                dma((groups, chunks)), dma((groups, chunks)),
                dma((groups, chunks)), dma((groups, chunks)),
                dma((groups, chunks)), dma((groups, chunks)),
                dma((planes,)), dma((planes,)), dma((planes,)), dma((planes,)),
                dma((groups,)), dma((groups,)), dma((groups,)), dma((groups,)),
            ],
            compiler_params=pltpu.CompilerParams(
                collective_id=0, has_side_effects=True, vmem_limit_bytes=56 * 1024 * 1024
            ),
        )(trailing, panel, inv_factor, later_series, fold_series, fold_len.reshape(1, series))

    in_specs = (
        P("row", "col"),
        P(("row", "col"), None),
        P(None, "col"),
        P("row", "col"),
        P("row", "col"),
        P("col"),
    )
    out_specs = (P("row", "col"), P("row", "col"))
    return jax.shard_map(
        on_device, mesh=mesh, in_specs=in_specs, out_specs=out_specs, check_vma=False
    )
```

```python
import functools

import jax
import jax.numpy as jnp
from jax import lax
from jax.experimental import pallas as pl
from jax.experimental.pallas import tpu as pltpu
from jax.sharding import PartitionSpec as P

MESH = pl.DeviceIdType.MESH
F32 = jnp.float32
BF16 = jnp.bfloat16
NT = (((1,), (1,)), ((), ()))
NN = (((1,), (0,)), ((), ()))


def split(x):
    high = x.astype(BF16)
    return high, (x - high.astype(F32)).astype(BF16)


def dot3(a, b, dims):
    dot = functools.partial(lax.dot_general, dimension_numbers=dims, preferred_element_type=F32)
    return dot(a[0], b[0]) + (dot(a[0], b[1]) + dot(a[1], b[0]))


def kernel(
    planes, groups, chunks,
    trailing_ref, panel_ref, inv_ref, later_ref, fold_ref, len_ref,
    out_ref, series_ref,
    tiles, inv_in, inv_t, fold, lens, q_hi, q_lo, g_hi, g_lo, local,
    rb_send, rb_recv, up_send, up_recv, sib_send, sib_recv,
    fold_send, fold_recv, fsib_send, fsib_recv,
    inv_send, inv_recv, isib_send, isib_recv,
):
    row = lax.axis_index("row")
    c = lax.axis_index("col")
    z = row // 2
    k = row % 2
    piece = panel_ref.shape[0]
    step = piece // chunks
    width = panel_ref.shape[1]
    fold_rows = fold_ref.shape[0]
    inv_cols = inv_ref.shape[1]
    half = inv_cols // 2
    sibling = (2 * z + (1 - k), c)

    barrier = pltpu.get_barrier_semaphore()
    pl.semaphore_signal(barrier, inc=1, device_id=sibling, device_id_type=MESH)
    for o in range(1, planes):
        pl.semaphore_signal(
            barrier, inc=1, device_id=(2 * ((z + o) % planes) + k, c), device_id_type=MESH
        )
    for o in range(1, groups):
        pl.semaphore_signal(
            barrier, inc=1, device_id=(row, (c + o) % groups), device_id_type=MESH
        )

    def slot_of(col):
        return jnp.where(col == z, k, 2)

    slot = slot_of(c)

    def rows_of(j, h):
        return pl.ds(pl.multiple_of(j * piece + h * step, step), step)

    def rb_copy(o, h):
        target = (c + o) % groups
        return pltpu.make_async_remote_copy(
            src_ref=tiles.at[slot, rows_of(c, h)],
            dst_ref=tiles.at[slot_of(target), rows_of(c, h)],
            send_sem=rb_send.at[o, h],
            recv_sem=rb_recv.at[c, h],
            device_id=(row, target),
            device_id_type=MESH,
        )

    def rb_arrival(j, h):
        return pltpu.make_async_remote_copy(
            src_ref=tiles.at[slot, rows_of(j, h)],
            dst_ref=tiles.at[slot, rows_of(j, h)],
            send_sem=rb_send.at[0, h],
            recv_sem=rb_recv.at[j, h],
            device_id=sibling,
            device_id_type=MESH,
        )

    def up_copy(j, h):
        return pltpu.make_async_remote_copy(
            src_ref=tiles.at[k, rows_of(j, h)],
            dst_ref=tiles.at[k, rows_of(j, h)],
            send_sem=up_send.at[j, h],
            recv_sem=up_recv.at[j, h],
            device_id=(jnp.minimum(row + 2, 2 * planes - 2 + k), c),
            device_id_type=MESH,
        )

    def sib_copy(tile, j, h):
        return pltpu.make_async_remote_copy(
            src_ref=tiles.at[tile, rows_of(j, h)],
            dst_ref=tiles.at[tile, rows_of(j, h)],
            send_sem=sib_send.at[j, h],
            recv_sem=sib_recv.at[j, h],
            device_id=sibling,
            device_id_type=MESH,
        )

    def fold_at(plane, core):
        return fold.at[pl.ds(pl.multiple_of((2 * plane + core) * fold_rows, fold_rows), fold_rows)]

    def fold_copy(o):
        target = (z + o) % planes
        return pltpu.make_async_remote_copy(
            src_ref=fold_at(z, k),
            dst_ref=fold_at(z, k),
            send_sem=fold_send.at[o],
            recv_sem=fold_recv.at[planes - o],
            device_id=(2 * target + k, c),
            device_id_type=MESH,
        )

    def fold_arrival(o):
        ref = fold_at((z + o) % planes, k)
        return pltpu.make_async_remote_copy(
            src_ref=ref, dst_ref=ref, send_sem=fold_send.at[0], recv_sem=fold_recv.at[o],
            device_id=sibling, device_id_type=MESH,
        )

    def fsib_copy(o, core):
        ref = fold_at((z + o) % planes, core)
        return pltpu.make_async_remote_copy(
            src_ref=ref, dst_ref=ref, send_sem=fsib_send.at[o], recv_sem=fsib_recv.at[o],
            device_id=sibling, device_id_type=MESH,
        )

    def inv_at(col, core):
        return inv_t.at[pl.ds(pl.multiple_of(col * inv_cols + core * half, half), half)]

    def inv_copy(o):
        return pltpu.make_async_remote_copy(
            src_ref=inv_at(c, k),
            dst_ref=inv_at(c, k),
            send_sem=inv_send.at[o],
            recv_sem=inv_recv.at[groups - o],
            device_id=(row, (c + o) % groups),
            device_id_type=MESH,
        )

    def inv_arrival(o):
        ref = inv_at((c + o) % groups, k)
        return pltpu.make_async_remote_copy(
            src_ref=ref, dst_ref=ref, send_sem=inv_send.at[0], recv_sem=inv_recv.at[o],
            device_id=sibling, device_id_type=MESH,
        )

    def isib_copy(o, core):
        ref = inv_at((c + o) % groups, core)
        return pltpu.make_async_remote_copy(
            src_ref=ref, dst_ref=ref, send_sem=isib_send.at[o], recv_sem=isib_recv.at[o],
            device_id=sibling, device_id_type=MESH,
        )

    has_tiles = z >= c
    relays = has_tiles & (z + 1 < planes)
    gives = (z > c) | ((z == c) & (k == 0))
    takes = (z > c) | ((z == c) & (k == 1))

    own = pl.ds(pl.multiple_of(c * piece, piece), piece)
    fetches = [
        pltpu.make_async_copy(src, dst, local.at[n])
        for n, (src, dst) in enumerate((
            (panel_ref, tiles.at[slot, own]),
            (fold_ref, fold_at(z, k)),
            (inv_ref, inv_in),
            (trailing_ref, out_ref),
            (later_ref, series_ref),
            (len_ref, lens),
        ))
    ]
    for fetch in fetches:
        fetch.start()
    pl.semaphore_wait(barrier, planes + groups - 1)

    def chain(j):
        for h in range(chunks):
            @pl.when(z > c)
            def _():
                up_copy(j, h).wait_recv()

            @pl.when((z == c) & (c != j))
            def _():
                rb_arrival(j, h).wait_recv()

            @pl.when(relays)
            def _():
                up_copy(j, h).start()

            @pl.when(gives)
            def _():
                sib_copy(k, j, h).start()

    ordered = (z < groups) & (z != c) & (z + 1 < planes)

    def is_first(o):
        return ordered & ((c + o) % groups == z)

    fetches[0].wait()
    for o in range(1, groups):
        @pl.when(is_first(o))
        def _():
            for h in range(chunks):
                rb_copy(o, h).start()

    fetches[1].wait()
    fsib_copy(0, k).start()
    for o in range(1, planes):
        fold_copy(o).start()
    fetches[2].wait()
    inv_t[pl.ds(pl.multiple_of(c * inv_cols, inv_cols), inv_cols), :] = inv_in[...].T

    for h in range(chunks):
        for o in range(1, groups):
            @pl.when(jnp.logical_not(is_first(o)))
            def _():
                rb_copy(o, h).start()
    for o in range(1, groups):
        @pl.when(jnp.logical_not(is_first(o)))
        def _():
            inv_copy(o).start()

    def send_last():
        for o in range(1, groups):
            @pl.when(is_first(o))
            def _():
                for h in range(chunks):
                    rb_copy(o, h).wait_send()
                inv_copy(o).start()

    below = z > c

    top = below & (z + 1 >= planes)

    def relay(first, last, where=below):
        @pl.when(where)
        def _():
            for j in range(first, last):
                chain(j)

    @pl.when(z == c)
    def _():
        for j in range(groups):
            chain(j)

    @pl.when(jnp.logical_not(below))
    def _():
        send_last()

    per = max(1, min(groups, 256 // piece))
    halfway = groups // 2

    def products(first, last):
        size = (last - first) * piece
        for which in range(2):
            tile = k if which == 0 else 1 - k
            active = has_tiles if which == 0 else takes

            @pl.when(active)
            def _():
                if which == 1:
                    for j in range(first, last):
                        for h in range(chunks):
                            sib_copy(1 - k, j, h).wait_recv()
                part = split(tiles[tile, first * piece : last * piece, :])
                at = pl.ds(pl.multiple_of(tile * (groups * piece) + first * piece, size), size)
                out_ref[:, at] = out_ref[:, at] - dot3((q_hi[...], q_lo[...]), part, NT)

    relay(0, halfway // 2)

    @pl.when(below)
    def _():
        send_last()

    for o in range(1, planes):
        fold_arrival(o).wait_recv()
        fsib_copy(o, k).start()
    relay(halfway // 2, halfway)
    relay(halfway, halfway + halfway // 2, below & relays)
    for o in range(1, groups):
        inv_arrival(o).wait_recv()
        isib_copy(o, k).start()
    for o in range(1, groups):
        isib_copy(o, 1 - k).wait_recv()
    inverse = split(inv_t[...])
    g_hi[...], g_lo[...] = split(dot3(inverse, inverse, NT))
    relay(halfway + halfway // 2, groups, below & relays)
    relay(halfway, halfway + halfway // 2, top)
    for j in range(groups):
        @pl.when((z != c) & (c != j))
        def _():
            for h in range(chunks):
                rb_arrival(j, h).wait_recv()
    q_hi[...], q_lo[...] = split(dot3(split(tiles[slot]), (g_hi[...], g_lo[...]), NN))
    for o in range(planes):
        fsib_copy(o, 1 - k).wait_recv()
    correction = dot3((q_hi[...], q_lo[...]), split(fold[...]), NN)
    for fetch in fetches[3:]:
        fetch.wait()
    later = series_ref[...]
    series_ref[...] = jnp.where(row < lens[...], later - correction, later)
    done = halfway + halfway // 2
    ready = (done // per) * per
    for first in range(0, ready, per):
        products(first, first + per)
    relay(done, groups, top)
    for first in range(ready, groups, per):
        products(first, min(first + per, groups))

    for o in range(1, groups):
        @pl.when(jnp.logical_not(is_first(o)))
        def _():
            for h in range(chunks):
                rb_copy(o, h).wait_send()
    for o in range(1, planes):
        fold_copy(o).wait_send()
    for o in range(planes):
        fsib_copy(o, k).wait_send()
    for o in range(1, groups):
        inv_copy(o).wait_send()
        isib_copy(o, k).wait_send()

    @pl.when(relays)
    def _():
        for j in range(groups):
            for h in range(chunks):
                up_copy(j, h).wait_send()

    @pl.when(gives)
    def _():
        for j in range(groups):
            for h in range(chunks):
                sib_copy(k, j, h).wait_send()


def solution(mesh):
    rows_axis = mesh.shape["row"]
    groups = mesh.shape["col"]
    planes = rows_axis // 2
    chunks = 4

    def on_device(trailing, panel, inv_factor, later_series, fold_series, fold_len):
        rows_here, cols_here = trailing.shape
        piece, width = panel.shape
        series = fold_series.shape[1]
        assert rows_axis % 2 == 0 and cols_here == 2 * rows_here and groups <= planes
        dma = pltpu.SemaphoreType.DMA
        vmem = pl.BlockSpec(memory_space=pltpu.VMEM)
        return pl.pallas_call(
            functools.partial(kernel, planes, groups, chunks),
            out_shape=(
                jax.ShapeDtypeStruct((rows_here, cols_here), F32),
                jax.ShapeDtypeStruct((rows_here, series), F32),
            ),
            in_specs=[pl.BlockSpec(memory_space=pltpu.HBM)] * 6,
            out_specs=(vmem, vmem),
            scratch_shapes=[
                pltpu.VMEM((3, rows_here, width), F32),
                pltpu.VMEM(inv_factor.shape, F32),
                pltpu.VMEM((width, width), F32),
                pltpu.VMEM((width, series), F32),
                pltpu.VMEM((1, series), jnp.int32),
                pltpu.VMEM((rows_here, width), BF16),
                pltpu.VMEM((rows_here, width), BF16),
                pltpu.VMEM((width, width), BF16),
                pltpu.VMEM((width, width), BF16),
                dma((6,)),
                dma((groups, chunks)), dma((groups, chunks)),
                dma((groups, chunks)), dma((groups, chunks)),
                dma((groups, chunks)), dma((groups, chunks)),
                dma((planes,)), dma((planes,)), dma((planes,)), dma((planes,)),
                dma((groups,)), dma((groups,)), dma((groups,)), dma((groups,)),
            ],
            compiler_params=pltpu.CompilerParams(
                collective_id=0, has_side_effects=True, vmem_limit_bytes=56 * 1024 * 1024
            ),
        )(trailing, panel, inv_factor, later_series, fold_series, fold_len.reshape(1, series))

    in_specs = (
        P("row", "col"),
        P(("row", "col"), None),
        P(None, "col"),
        P("row", "col"),
        P("row", "col"),
        P("col"),
    )
    out_specs = (P("row", "col"), P("row", "col"))
    return jax.shard_map(
        on_device, mesh=mesh, in_specs=in_specs, out_specs=out_specs, check_vma=False
    )
```
